32 devices in a mesh: section: 2 (over y), dp: 2 (over x), seq: 8 (over z, core).
Axes of the slice: x: 2, y: 2, z: 4, core: 2. Of those that a mesh axis runs over, the one named last changes fastest.
Arguments:
- ends: bfloat16 [2, 8, 1024, 960], P('section', 'dp', 'seq'), may hold values from -6 to 6
- segments: int32 [8, 1024], P('dp', 'seq'), may hold values from 0 to 7, as said below
- positions: int32 [8, 1024], P('dp', 'seq'), may hold values from 0 to 1023, as said below
- query_weights: bfloat16 [2, 960, 960], P('section', 'dp', 'seq'), may hold values from -0.1875 to 0.1875
- key_weights: bfloat16 [2, 960, 320], P('section', 'dp', 'seq'), may hold values from -0.1875 to 0.1875
- value_weights: bfloat16 [2, 960, 320], P('section', 'dp', 'seq'), may hold values from -0.1875 to 0.1875
- out_weights: bfloat16 [2, 960, 960], P('section', 'seq', 'dp'), may hold values from -1.25 to 1.25
- gate_weights: bfloat16 [2, 960, 2560], P('section', 'dp', 'seq'), may hold values from -0.1875 to 0.1875
- up_weights: bfloat16 [2, 960, 2560], P('section', 'dp', 'seq'), may hold values from -0.1875 to 0.1875
- down_weights: bfloat16 [2, 2560, 960], P('section', 'seq', 'dp'), may hold values from -0.125 to 0.125
- norm_gains: bfloat16 [2, 2, 960], P('section', None, 'seq'), may hold values from 0.099609375 to 1.8984375
Outputs:
- activations: bfloat16 [2, 8, 1024, 960], P('section', 'dp', 'seq')
- input_grads: bfloat16 [2, 8, 1024, 960], P('section', 'dp', 'seq')
- query_grad: float32 [2, 960, 960], P('section', 'dp', 'seq')
- key_grad: float32 [2, 960, 320], P('section', 'dp', 'seq')
- value_grad: float32 [2, 960, 320], P('section', 'dp', 'seq')
- out_grad: float32 [2, 960, 960], P('section', 'seq', 'dp')
- gate_grad: float32 [2, 960, 2560], P('section', 'dp', 'seq')
- up_grad: float32 [2, 960, 2560], P('section', 'dp', 'seq')
- down_grad: float32 [2, 2560, 960], P('section', 'seq', 'dp')
- gain_grad: float32 [2, 2, 960], P('section', None, 'seq')
The draws below stay inside these ranges and needn't reach their ends.
Inputs may be any that keep to these rules, and one draw needn't show every extreme that they name: `segments`: within each sequence the ids start at 0 and rise by 0 or 1 from one position to the next, so equal ids form one document; among the 4 sequences of each index of dp, one is a single document and another holds 8 documents. `positions`: 0 at a document's first token, rising by 1 a token within it.
All inputs are finite; a program needn't handle non-finite values.
Results may differ from the reference program's by a relative error of at most 0.025.
Values may be sent and summed in bfloat16 or wider, within the bound.
A program may use at most 256 MiB of HBM per device.

```python
import math
import jax
import jax.numpy as jnp
from jax import lax

D = 960
HEADS = 15
KV_HEADS = 5
HEAD_DIM = 64
FF = 2560
SEQ_MB = 2
MICRO = 2
LEN = 1024
SEQS = 8
N_SECTION = 2


def documents(key):
    unit = LEN // 8
    group = MICRO * SEQ_MB
    first, second, third = jax.random.split(key, 3)
    offsets = jax.random.randint(first, (SEQS, 7), 0, unit // 2)
    active = jax.random.randint(second, (SEQS, 7), 0, 2)
    chosen = jax.random.randint(third, (SEQS // group, 1), 0, group)
    members = jnp.arange(group)[None, :]
    single = (members == chosen).reshape(SEQS)
    crowded = (members == (chosen + 1) % group).reshape(SEQS)
    active = jnp.where(crowded[:, None], 1, active)
    active = jnp.where(single[:, None], 0, active)
    starts = (jnp.arange(1, 8) * unit)[None, :] + offsets
    places = jnp.arange(LEN)
    flags = jnp.sum(active[:, :, None] * (places[None, None, :] == starts[:, :, None]).astype(jnp.int32), axis=1)
    segment = jnp.cumsum(flags, axis=1).astype(jnp.int32)
    begins = lax.cummax(places[None, :] * flags, axis=1)
    return (segment, (places[None, :] - begins).astype(jnp.int32))


def draw_segments(key, part):
    segment, places = documents(key)
    return segment


def draw_positions(key, part):
    segment, places = documents(key)
    return places


def block_scale(rng, dims, pieces, low, largest):
    level, own = 1.0, jax.random.fold_in(rng, 6)
    for position, blocks in pieces:
        heights = jnp.exp(jax.random.uniform(jax.random.fold_in(own, position), (blocks,), jnp.float32, low / len(pieces), largest / len(pieces)))
        level = level * jnp.repeat(heights, dims[position] // blocks).reshape([-1 if axis == position else 1 for axis in range(len(dims))])
    return level


def bell_draw(key, shape, width, bound, pieces=(), kind=jnp.bfloat16):
    result = jax.random.normal(key, shape, jnp.float32) * width
    if len(pieces) > 0:
        result = block_scale(key, shape, pieces, -0.22, 0.18) * result
    return jnp.clip(result, min=-bound, max=bound).astype(kind)


def setup_inputs(seed: int = 0) -> dict:
    splits = jax.random.split(jax.random.key(seed), 12)
    ends = bell_draw(splits[0], (2, SEQS, LEN, D), 1.0, 6.0, ((0, 2), (1, 2), (2, 8)))
    segments = draw_segments(jax.random.fold_in(splits[11], 71), 0)
    positions = draw_positions(jax.random.fold_in(splits[11], 71), 0)
    query_weights = bell_draw(splits[3], (N_SECTION, D, HEADS * HEAD_DIM), D ** -0.5, 0.1875, ((0, 2), (1, 2), (2, 8)))
    key_weights = bell_draw(splits[4], (N_SECTION, D, KV_HEADS * HEAD_DIM), D ** -0.5, 0.1875, ((0, 2), (1, 2), (2, 8)))
    value_weights = bell_draw(splits[5], (N_SECTION, D, KV_HEADS * HEAD_DIM), D ** -0.5, 0.1875, ((0, 2), (1, 2), (2, 8)))
    out_weights = bell_draw(splits[6], (N_SECTION, HEADS * HEAD_DIM, D), (D // 40) ** -0.5, 1.25, ((0, 2), (1, 8), (2, 2)))
    gate_weights = bell_draw(splits[7], (N_SECTION, D, FF), D ** -0.5, 0.1875, ((0, 2), (1, 2), (2, 8)))
    up_weights = bell_draw(splits[8], (N_SECTION, D, FF), D ** -0.5, 0.1875, ((0, 2), (1, 2), (2, 8)))
    down_weights = bell_draw(splits[9], (N_SECTION, FF, D), FF ** -0.5, 0.125, ((0, 2), (1, 8), (2, 2)))
    norm_gains = jnp.clip(1.0 + 0.18 * jax.random.normal(splits[10], (N_SECTION, 2, D), jnp.float32), 0.099609375, 1.8984375).astype(jnp.bfloat16)
    return {"ends": ends, "segments": segments, "positions": positions, "query_weights": query_weights, "key_weights": key_weights, "value_weights": value_weights, "out_weights": out_weights, "gate_weights": gate_weights, "up_weights": up_weights, "down_weights": down_weights, "norm_gains": norm_gains}


EPS = 1e-05
THETA = 100000.0
MASKED = -1e+30

@jax.custom_vjp
def low(v):
    return lax.optimization_barrier(v.astype(jnp.bfloat16)).astype(jnp.float32)

@jax.custom_vjp
def low_back(v):
    return v

def low_keep(v):
    return (low(v), None)

def low_pass(kept, grad):
    return (grad,)

def back_keep(v):
    return (v, None)

def back_low(kept, grad):
    return (low(grad),)
low.defvjp(low_keep, low_pass)
low_back.defvjp(back_keep, back_low)

def rope_tables(positions):
    half_size = HEAD_DIM // 2
    exponent = jnp.arange(half_size, dtype=jnp.float32) * (2.0 / HEAD_DIM)
    frequency = jnp.exp(-exponent * math.log(THETA))
    angles = positions.astype(jnp.float32)[..., None] * frequency
    return (jnp.cos(angles), jnp.sin(angles))

def rotate(values, cosine, sine):
    front, back = jnp.split(values, 2, axis=-1)
    cosine = cosine[..., None, :]
    sine = sine[..., None, :]
    return jnp.concatenate([front * cosine - back * sine, back * cosine + front * sine], axis=-1)

def dense(values, weight):
    return jnp.dot(values, weight, preferred_element_type=jnp.float32, precision=lax.Precision.HIGHEST)

def norm(values, gain):
    scale = lax.rsqrt(lax.optimization_barrier(jnp.mean(values * values, axis=-1, keepdims=True)) + EPS)
    return values * scale * gain

def sequence_attention(items):
    queries, keys, values, segment = items
    length = queries.shape[0]
    grouped = queries.reshape(length, KV_HEADS, HEADS // KV_HEADS, HEAD_DIM)
    scores = jnp.einsum('qgrd,kgd->grqk', grouped, keys, precision=lax.Precision.HIGHEST) * HEAD_DIM ** (-0.5)
    scores = low_back(scores)
    index = jnp.arange(length)
    allowed = (index[None, :] <= index[:, None]) & (segment[None, :] == segment[:, None])
    scores = jnp.where(allowed, scores, MASKED)
    top = lax.optimization_barrier(jnp.max(scores, axis=-1, keepdims=True))
    weights = jnp.exp(scores - top)
    shares = low(weights / lax.optimization_barrier(jnp.sum(weights, axis=-1, keepdims=True)))
    mixed = jnp.einsum('grqk,kgd->qgrd', shares, values, precision=lax.Precision.HIGHEST)
    return mixed.reshape(length, HEADS * HEAD_DIM)

def layer(hidden, weights, segments, cosine, sine):
    query_weight, key_weight, value_weight, out_weight, gate_weight, up_weight, down_weight, gains = weights
    count, length = segments.shape
    normed = low(norm(hidden, gains[0]))
    queries = low_back(dense(normed, query_weight))
    keys = low_back(dense(normed, key_weight))
    values = low_back(low(dense(normed, value_weight)))
    turned_queries = low(rotate(queries.reshape(count, length, HEADS, HEAD_DIM), cosine, sine))
    turned_keys = low(rotate(keys.reshape(count, length, KV_HEADS, HEAD_DIM), cosine, sine))
    values = values.reshape(count, length, KV_HEADS, HEAD_DIM)
    mixed = lax.map(jax.checkpoint(sequence_attention), (turned_queries, turned_keys, values, segments))
    mixed = low_back(low(mixed))
    middle = hidden + low_back(dense(mixed, out_weight))
    normed_back = low(norm(middle, gains[1]))
    gate = low_back(dense(normed_back, gate_weight))
    upward = low_back(dense(normed_back, up_weight))
    product = low(gate * jax.nn.sigmoid(gate) * upward)
    return middle + dense(product, down_weight)

def reference(ends, segments, positions, query_weights, key_weights, value_weights, out_weights, gate_weights, up_weights, down_weights, norm_gains):
    inputs = ends[0].astype(jnp.float32)
    cotangent = ends[1].astype(jnp.float32)
    params = (query_weights.astype(jnp.float32), key_weights.astype(jnp.float32), value_weights.astype(jnp.float32), out_weights.astype(jnp.float32), gate_weights.astype(jnp.float32), up_weights.astype(jnp.float32), down_weights.astype(jnp.float32), norm_gains.astype(jnp.float32))
    cosine, sine = rope_tables(positions)
    probes = jnp.zeros((N_SECTION,) + inputs.shape, jnp.float32)

    def forward(params, inputs, probes):
        hidden = inputs + probes[0]
        stored = []
        for level in range(N_SECTION):
            if level > 0:
                hidden = low_back(low(hidden) + probes[level])
            hidden = layer(hidden, tuple((weight[level] for weight in params)), segments, cosine, sine)
            stored.append(low(hidden))
        return (hidden, jnp.stack(stored))
    output, pullback, stored = jax.vjp(forward, params, inputs, probes, has_aux=True)
    grads, input_grad, probe_grads = pullback(cotangent)
    activations = stored.astype(jnp.bfloat16)
    input_grads = probe_grads.astype(jnp.bfloat16)
    return (activations, input_grads, grads[0], grads[1], grads[2], grads[3], grads[4], grads[5], grads[6], grads[7])
```

```python
import math

import jax
import jax.numpy as jnp
from jax import lax
from jax.sharding import PartitionSpec as P

D = 960
HEADS = 15
KV_HEADS = 5
HEAD_DIM = 64
SEQ_MB = 2


EPS = 1e-05
THETA = 100000.0
MASKED = -1e30


def shifted(value, axis, steps):
    count = lax.axis_size(axis)
    leading, last = (max(0, -steps), min(count, count - steps))
    return lax.ppermute(value, axis, [(source, source + steps) for source in range(leading, last)])


def rope_tables(positions):
    half_size = HEAD_DIM // 2
    exponent = jnp.arange(half_size, dtype=jnp.float32) * (2.0 / HEAD_DIM)
    frequency = jnp.exp(-exponent * math.log(THETA))
    angles = positions.astype(jnp.float32)[..., None] * frequency
    return (jnp.cos(angles), jnp.sin(angles))


def inner_rows(left, right):
    return lax.dot_general(
        left, right, (((0,), (0,)), ((), ())), preferred_element_type=jnp.float32
    )


def against(left, weight):
    return lax.dot_general(
        left, weight, (((1,), (1,)), ((), ())), preferred_element_type=jnp.float32
    )


def normalize(values, gain):
    scale = lax.rsqrt(jnp.mean(values * values, axis=-1, keepdims=True) + EPS)
    return (scale, (values * scale * gain).astype(jnp.bfloat16))


def norm_back(gradient, values, scale, gain):
    weighted = gradient * gain
    inward = scale * weighted - values * (scale * scale * scale) * jnp.mean(
        weighted * values, axis=-1, keepdims=True
    )
    return (inward, jnp.sum(gradient * values * scale, axis=0))


def key_slice(gathered, segment_all, begin, width):
    count = gathered.shape[0]
    key_width = KV_HEADS * HEAD_DIM
    block = lax.dynamic_slice_in_dim(gathered, begin, width, 1)
    segment_block = lax.dynamic_slice_in_dim(segment_all, begin, width, 1)
    keys = block[..., :key_width].reshape(count, width, KV_HEADS, HEAD_DIM)
    values = block[..., key_width:].reshape(count, width, KV_HEADS, HEAD_DIM)
    return (keys, values, segment_block)


def masked_scores(query_view, keys, segment_block, segment_mark, query_index, begin):
    width = keys.shape[1]
    scores = jnp.einsum(
        "sqgrd,skgd->sgrqk", query_view, keys, preferred_element_type=jnp.float32
    ) * HEAD_DIM ** (-0.5)
    key_index = begin + jnp.arange(width)
    allowed = (key_index[None, None, :] <= query_index[None, :, None]) & (
        segment_block[:, None, :] == segment_mark[:, :, None]
    )
    return jnp.where(allowed[:, None, None], scores, MASKED)


def block_width():
    return 512


def attend(query_view, gathered, segment_all, segment_mark, query_index):
    count, local_length, groups, ratio, head_size = query_view.shape
    key_length = gathered.shape[1]
    width = block_width()
    blocks = key_length // width
    row_shape = (count, groups, ratio, local_length)

    def measure(index, carry):
        top, total = carry
        begin = index * width
        keys, values, segment_block = key_slice(gathered, segment_all, begin, width)
        scores = masked_scores(query_view, keys, segment_block, segment_mark, query_index, begin)
        new_top = jnp.maximum(top, jnp.max(scores, axis=-1))
        total = total * jnp.exp(top - new_top) + jnp.sum(
            jnp.exp(scores - new_top[..., None]), axis=-1
        )
        return (new_top, total)

    start = (jnp.full(row_shape, MASKED, jnp.float32), jnp.zeros(row_shape, jnp.float32))
    top, total = lax.fori_loop(0, blocks, measure, start)
    log_total = top + jnp.log(total)

    def gather_mix(index, running):
        begin = index * width
        keys, values, segment_block = key_slice(gathered, segment_all, begin, width)
        scores = masked_scores(query_view, keys, segment_block, segment_mark, query_index, begin)
        shares = jnp.exp(scores - log_total[..., None]).astype(jnp.bfloat16)
        return running + jnp.einsum(
            "sgrqk,skgd->sqgrd", shares, values, preferred_element_type=jnp.float32
        )

    mixed = lax.fori_loop(0, blocks, gather_mix, jnp.zeros(query_view.shape, jnp.float32))
    return (mixed, log_total)


def attend_back(
    query_view, gathered, segment_all, segment_mark, query_index, log_total, back_view, delta
):
    count = query_view.shape[0]
    key_length = gathered.shape[1]
    key_width = KV_HEADS * HEAD_DIM
    width = block_width()
    blocks = key_length // width
    scale = HEAD_DIM ** (-0.5)

    def sweep(index, carry):
        back_query, buffer = carry
        begin = index * width
        keys, values, segment_block = key_slice(gathered, segment_all, begin, width)
        scores = masked_scores(query_view, keys, segment_block, segment_mark, query_index, begin)
        shares = jnp.exp(scores - log_total[..., None])
        back_shares = jnp.einsum(
            "sqgrd,skgd->sgrqk", back_view, values, preferred_element_type=jnp.float32
        )
        back_scores = (shares * (back_shares - delta[..., None])).astype(jnp.bfloat16)
        back_values = jnp.einsum(
            "sgrqk,sqgrd->skgd",
            shares.astype(jnp.bfloat16),
            back_view,
            preferred_element_type=jnp.float32,
        )
        back_keys = (
            jnp.einsum(
                "sgrqk,sqgrd->skgd", back_scores, query_view, preferred_element_type=jnp.float32
            )
            * scale
        )
        back_query = (
            back_query
            + jnp.einsum("sgrqk,skgd->sqgrd", back_scores, keys, preferred_element_type=jnp.float32)
            * scale
        )
        piece = jnp.concatenate(
            [
                back_keys.reshape(count, width, key_width),
                back_values.reshape(count, width, key_width),
            ],
            axis=-1,
        )
        return (back_query, lax.dynamic_update_slice_in_dim(buffer, piece, begin, 1))

    start = (
        jnp.zeros(query_view.shape, jnp.float32),
        jnp.zeros((count, key_length, 2 * key_width), jnp.float32),
    )
    return lax.fori_loop(0, blocks, sweep, start)


def swap_halves(values):
    half = HEAD_DIM // 2
    width = values.shape[-1]
    lane = lax.broadcasted_iota(jnp.int32, values.shape, 1) % HEAD_DIM
    ahead = jnp.concatenate([values[:, half:], values[:, :half]], axis=1)
    behind = jnp.concatenate([values[:, width - half :], values[:, : width - half]], axis=1)
    return jnp.where(lane < half, ahead, behind)


def turn(values, cosine, sine):
    copies = values.shape[-1] // HEAD_DIM
    return values * jnp.tile(cosine, (1, copies)) + swap_halves(values) * jnp.tile(
        sine, (1, copies)
    )


def layer_forward(hidden, full, segment_mark, segment_all, cosine, sine, query_index):
    qkv_weight, out_weight, gate_up_weight, down_weight, gains = full
    count, local_length = segment_mark.shape
    rows = hidden.shape[0]
    key_width = KV_HEADS * HEAD_DIM
    query_width = HEADS * HEAD_DIM
    scale_front, normed = normalize(hidden, gains[0])
    qkv = against(normed, qkv_weight)
    turned = turn(qkv[:, : query_width + key_width], cosine, sine).astype(jnp.bfloat16)
    values = qkv[:, query_width + key_width :].astype(jnp.bfloat16)
    packed = jnp.concatenate([turned[:, query_width:], values], axis=-1)
    gathered = lax.all_gather(
        packed.reshape(count, local_length, 2 * key_width), "seq", axis=1, tiled=True
    )
    query_view = turned[:, :query_width].reshape(
        count, local_length, KV_HEADS, HEADS // KV_HEADS, HEAD_DIM
    )
    mixed, log_total = attend(query_view, gathered, segment_all, segment_mark, query_index)
    mixed_low = mixed.reshape(rows, query_width).astype(jnp.bfloat16)
    middle = hidden + jnp.dot(mixed_low, out_weight, preferred_element_type=jnp.float32)
    scale_back, normed_back = normalize(middle, gains[1])
    gate_up = against(normed_back, gate_up_weight)
    width = gate_up.shape[1] // 2
    gate, upward = gate_up[:, :width], gate_up[:, width:]
    product = (gate * jax.nn.sigmoid(gate) * upward).astype(jnp.bfloat16)
    output = middle + jnp.dot(product, down_weight, preferred_element_type=jnp.float32)
    kept = (
        hidden,
        scale_front,
        normed,
        query_view,
        gathered,
        mixed,
        log_total,
        mixed_low,
        middle,
        scale_back,
        normed_back,
        gate_up,
        product,
    )
    return (output, kept)


def layer_backward(incoming_low, full, kept, segment_mark, segment_all, cosine, sine, query_index):
    qkv_weight, out_weight, gate_up_weight, down_weight, gains = full
    (
        hidden,
        scale_front,
        normed,
        query_view,
        gathered,
        mixed,
        log_total,
        mixed_low,
        middle,
        scale_back,
        normed_back,
        gate_up,
        product,
    ) = kept
    rows = hidden.shape[0]
    key_width = KV_HEADS * HEAD_DIM
    query_width = HEADS * HEAD_DIM
    width = gate_up.shape[1] // 2
    gate, upward = gate_up[:, :width], gate_up[:, width:]
    incoming = incoming_low.astype(jnp.float32)
    back_product = against(incoming_low, down_weight)
    sigma = jax.nn.sigmoid(gate)
    back_gate = (back_product * upward * sigma * (1.0 + gate * (1.0 - sigma))).astype(jnp.bfloat16)
    back_up = (back_product * gate * sigma).astype(jnp.bfloat16)
    back_gate_up = jnp.concatenate([back_gate, back_up], axis=1)
    back_normed = jnp.dot(back_gate_up, gate_up_weight, preferred_element_type=jnp.float32)
    inward, gain_back_grad = norm_back(back_normed, middle, scale_back, gains[1])
    back_middle = incoming + inward
    branch = back_middle.astype(jnp.bfloat16)
    back_mixed = against(branch, out_weight).astype(jnp.bfloat16)
    back_view = back_mixed.reshape(query_view.shape)
    delta = jnp.einsum("sqgrd,sqgrd->sgrq", back_view.astype(jnp.float32), mixed)
    back_query, buffer = attend_back(
        query_view, gathered, segment_all, segment_mark, query_index, log_total, back_view, delta
    )
    summed = lax.psum_scatter(
        buffer.astype(jnp.bfloat16), "seq", scatter_dimension=1, tiled=True
    ).reshape(rows, 2 * key_width)
    back_queries = turn(back_query.reshape(rows, query_width), cosine, -sine).astype(jnp.bfloat16)
    back_keys = turn(summed[:, :key_width].astype(jnp.float32), cosine, -sine).astype(jnp.bfloat16)
    back_qkv = jnp.concatenate([back_queries, back_keys, summed[:, key_width:]], axis=1)
    back_front = jnp.dot(back_qkv, qkv_weight, preferred_element_type=jnp.float32)
    inward_front, gain_front_grad = norm_back(back_front, hidden, scale_front, gains[0])
    back_hidden = back_middle + inward_front
    gains_grad = jnp.stack([gain_front_grad, gain_back_grad])
    terms = (normed, back_qkv, mixed_low, branch, normed_back, back_gate_up, product, incoming_low)
    return (back_hidden, terms, gains_grad)


GAIN_ROWS = 16


def gather_weights(shards):
    query_part, key_part, value_part, out_part, gate_part, up_part, down_part, gain_part = shards
    seq = lax.axis_size("seq")
    dp = lax.axis_size("dp")
    lanes = query_part.shape[0]
    heights = (query_part.shape[1], key_part.shape[1], value_part.shape[1], out_part.shape[0])
    gain_block = jnp.pad(
        gain_part, ((0, GAIN_ROWS - gain_part.shape[0]), (0, lanes - gain_part.shape[1]))
    )
    front = jnp.concatenate(
        [
            jnp.concatenate([query_part, key_part, value_part], axis=1).T,
            out_part,
            gain_block,
        ],
        axis=0,
    )
    rear = jnp.concatenate([jnp.concatenate([gate_part, up_part], axis=1).T, down_part], axis=0)
    front_all = lax.all_gather(front, ("seq", "dp"), axis=0, tiled=False)
    front_all = front_all.reshape(seq, dp, front.shape[0], lanes)
    rear_all = lax.all_gather(rear, ("seq", "dp"), axis=0, tiled=False)
    rear_all = rear_all.reshape(seq, dp, rear.shape[0], lanes)

    def whole(block, begin, size):
        piece = lax.slice_in_dim(block, begin, begin + size, axis=2)
        return piece.transpose(0, 2, 1, 3).reshape(seq * size, dp * lanes)

    places = [0]
    for height in heights:
        places.append(places[-1] + height)
    qkv = jnp.concatenate([whole(front_all, places[i], heights[i]) for i in range(3)], axis=0)
    out = whole(front_all, places[3], heights[3])
    gain_width = gain_part.shape[1]
    gains = lax.slice(
        front_all, (0, 0, places[4], 0), (seq, 1, places[4] + gain_part.shape[0], gain_width)
    )
    gains = gains[:, 0].transpose(1, 0, 2).reshape(gain_part.shape[0], seq * gain_width)
    step = gate_part.shape[1]
    gate_up = jnp.concatenate([whole(rear_all, 0, step), whole(rear_all, step, step)], axis=0)
    down = whole(rear_all, 2 * step, step)
    return (qkv, out, gate_up, down, gains.astype(jnp.float32))


def split_blocks(grad, seq, dp):
    rows, columns = grad.shape
    return grad.reshape(seq, rows // seq, dp, columns // dp).transpose(0, 2, 1, 3)


def scatter_sum(blocks):
    seq, dp, rows, lanes = blocks.shape
    return lax.psum_scatter(
        blocks.reshape(seq * dp * rows, lanes), ("seq", "dp"), scatter_dimension=0, tiled=True
    )


def reduce_grads(terms, gains_grad):
    normed, back_qkv, mixed_low, branch, normed_back, back_gate_up, product, incoming = terms
    seq = lax.axis_size("seq")
    dp = lax.axis_size("dp")
    key_width = KV_HEADS * HEAD_DIM
    query_width = HEADS * HEAD_DIM

    def outer(left, right):
        return inner_rows(left, right).astype(jnp.bfloat16)

    gate_up = outer(back_gate_up, normed_back)
    down = outer(product, incoming)
    hidden_width = down.shape[0]
    rear = jnp.concatenate(
        [
            split_blocks(gate_up[:hidden_width], seq, dp),
            split_blocks(gate_up[hidden_width:], seq, dp),
            split_blocks(down, seq, dp),
        ],
        axis=2,
    )
    rear = scatter_sum(rear).astype(jnp.float32)
    qkv = outer(back_qkv, normed)
    out = outer(mixed_low, branch)
    gain_kinds, gain_all = gains_grad.shape
    gain_width = gain_all // seq
    lanes = out.shape[1] // dp
    gain_block = gains_grad.astype(jnp.bfloat16).reshape(gain_kinds, seq, gain_width)
    gain_block = gain_block.transpose(1, 0, 2)
    gain_block = jnp.pad(
        gain_block, ((0, 0), (0, GAIN_ROWS - gain_kinds), (0, lanes - gain_width))
    )
    gain_block = jnp.broadcast_to(gain_block[:, None], (seq, dp, GAIN_ROWS, lanes))
    front = jnp.concatenate(
        [
            split_blocks(qkv[:query_width], seq, dp),
            split_blocks(qkv[query_width : query_width + key_width], seq, dp),
            split_blocks(qkv[query_width + key_width :], seq, dp),
            split_blocks(out, seq, dp),
            gain_block,
        ],
        axis=2,
    )
    front = scatter_sum(front).astype(jnp.float32)
    query_rows = query_width // seq
    key_rows = key_width // seq
    first = query_rows + key_rows
    second = first + key_rows
    third = second + query_rows
    hidden_rows = hidden_width // seq
    return (
        front[:query_rows].T,
        front[query_rows:first].T,
        front[first:second].T,
        front[second:third],
        rear[:hidden_rows].T,
        rear[hidden_rows : 2 * hidden_rows].T,
        rear[2 * hidden_rows :],
        front[third : third + gain_kinds, :gain_width],
    )


def pick_section(section, early, late):

    def select(early_part, late_part):
        return jnp.where(section == 0, early_part, late_part)

    return jax.tree.map(select, early, late)


def on_device(
    ends,
    segments,
    positions,
    query_weights,
    key_weights,
    value_weights,
    out_weights,
    gate_weights,
    up_weights,
    down_weights,
    norm_gains,
):
    section = lax.axis_index("section")
    sections = lax.axis_size("section")
    count = SEQ_MB
    micro = segments.shape[0] // count
    local_length = segments.shape[1]
    rows = count * local_length
    ticks = micro + sections - 1
    query_index = lax.axis_index("seq") * local_length + jnp.arange(local_length)
    shards = (
        query_weights[0],
        key_weights[0],
        value_weights[0],
        out_weights[0],
        gate_weights[0],
        up_weights[0],
        down_weights[0],
        norm_gains[0],
    )
    full = gather_weights(shards)
    outside = ends[0].reshape(micro, rows, D)
    blank = jnp.zeros((rows, D), jnp.bfloat16)

    marks = segments.astype(jnp.bfloat16)
    marks_all = lax.all_gather(marks, "seq", axis=1, tiled=True)
    cosines, sines = rope_tables(positions.reshape(micro * rows))
    cosines = jnp.concatenate([cosines, cosines], axis=1)
    sines = jnp.concatenate([-sines, sines], axis=1)

    def batch_inputs(index):
        mark = lax.dynamic_slice_in_dim(marks, index * count, count, 0)
        mark_all = lax.dynamic_slice_in_dim(marks_all, index * count, count, 0)
        cosine = lax.dynamic_slice_in_dim(cosines, index * rows, rows, 0)
        sine = lax.dynamic_slice_in_dim(sines, index * rows, rows, 0)
        return (mark, mark_all, cosine, sine)

    received = blank
    results = []
    stores = []
    for tick in range(ticks):
        own = outside[tick] if tick < micro else blank
        source = jnp.where(section == 0, own, received)
        index = jnp.clip(tick - section, 0, micro - 1)
        mark, mark_all, cosine, sine = batch_inputs(index)
        output, kept = layer_forward(
            source.astype(jnp.float32), full, mark, mark_all, cosine, sine, query_index
        )
        sent = output.astype(jnp.bfloat16)
        results.append(sent)
        stores.append(kept)
        if tick + 1 < ticks:
            received = shifted(sent, "section", 1)
    received = blank
    sent_back = []
    collected = []
    gains_grad = 0.0
    for tick in range(ticks):
        own = outside[tick] if tick < micro else blank
        incoming = jnp.where(section == sections - 1, own, received)
        index = jnp.clip(tick - 1 + section, 0, micro - 1)
        mark, mark_all, cosine, sine = batch_inputs(index)
        kept = pick_section(section, stores[max(tick - 1, 0)], stores[min(tick + 1, ticks - 1)])
        back_hidden, terms, gains_part = layer_backward(
            incoming, full, kept, mark, mark_all, cosine, sine, query_index
        )
        collected.append(terms)
        gains_grad = gains_grad + gains_part
        sent = back_hidden.astype(jnp.bfloat16)
        sent_back.append(sent)
        if tick + 1 < ticks:
            received = shifted(sent, "section", -1)
    terms = tuple(jnp.concatenate(parts, axis=0) for parts in zip(*collected))
    totals = reduce_grads(terms, gains_grad)
    outputs_list = []
    grads_list = []
    for batch in range(micro):
        outputs_list.append(
            jnp.where(section == 0, results[batch], results[batch + 1]).reshape(
                count, local_length, D
            )
        )
        grads_list.append(
            jnp.where(section == 0, sent_back[batch + 1], sent_back[batch]).reshape(
                count, local_length, D
            )
        )
    activations = jnp.concatenate(outputs_list, axis=0)[None]
    input_grads = jnp.concatenate(grads_list, axis=0)[None]
    return (
        activations,
        input_grads,
        totals[0][None],
        totals[1][None],
        totals[2][None],
        totals[3][None],
        totals[4][None],
        totals[5][None],
        totals[6][None],
        totals[7][None],
    )


def solution(mesh):
    return jax.shard_map(
        on_device,
        mesh=mesh,
        in_specs=(
            P("section", "dp", "seq", None),
            P("dp", "seq"),
            P("dp", "seq"),
            P("section", "dp", "seq"),
            P("section", "dp", "seq"),
            P("section", "dp", "seq"),
            P("section", "seq", "dp"),
            P("section", "dp", "seq"),
            P("section", "dp", "seq"),
            P("section", "seq", "dp"),
            P("section", None, "seq"),
        ),
        out_specs=(
            P("section", "dp", "seq", None),
            P("section", "dp", "seq", None),
            P("section", "dp", "seq"),
            P("section", "dp", "seq"),
            P("section", "dp", "seq"),
            P("section", "seq", "dp"),
            P("section", "dp", "seq"),
            P("section", "dp", "seq"),
            P("section", "seq", "dp"),
            P("section", None, "seq"),
        ),
        check_vma=False,
    )
```

```python
import math

import jax
import jax.numpy as jnp
from jax import lax
from jax.experimental import pallas as pl
from jax.experimental.pallas import tpu as pltpu
from jax.sharding import PartitionSpec as P

D = 960
HEADS = 15
KV_HEADS = 5
HEAD_DIM = 64
SEQ_MB = 2


EPS = 1e-05
THETA = 100000.0
MASKED = -1e30


def shifted(value, axis, steps):
    count = lax.axis_size(axis)
    leading, last = (max(0, -steps), min(count, count - steps))
    return lax.ppermute(value, axis, [(source, source + steps) for source in range(leading, last)])


def rope_tables(positions):
    half_size = HEAD_DIM // 2
    exponent = jnp.arange(half_size, dtype=jnp.float32) * (2.0 / HEAD_DIM)
    frequency = jnp.exp(-exponent * math.log(THETA))
    angles = positions.astype(jnp.float32)[..., None] * frequency
    return (jnp.cos(angles), jnp.sin(angles))


def inner_rows(left, right):
    return lax.dot_general(
        left, right, (((0,), (0,)), ((), ())), preferred_element_type=jnp.float32
    )


def against(left, weight):
    return lax.dot_general(
        left, weight, (((1,), (1,)), ((), ())), preferred_element_type=jnp.float32
    )


def normalize(values, gain):
    scale = lax.rsqrt(jnp.mean(values * values, axis=-1, keepdims=True) + EPS)
    return (scale, (values * scale * gain).astype(jnp.bfloat16))


def norm_back(gradient, values, scale, gain):
    weighted = gradient * gain
    inward = scale * weighted - values * (scale * scale * scale) * jnp.mean(
        weighted * values, axis=-1, keepdims=True
    )
    return (inward, jnp.sum(gradient * values * scale, axis=0))


RATIO = HEADS // KV_HEADS
KEY_WIDTH = KV_HEADS * HEAD_DIM


def stacked_heads(ref, group):
    begin = group * RATIO
    heads = [
        ref[0, :, (begin + head) * HEAD_DIM : (begin + head + 1) * HEAD_DIM]
        for head in range(RATIO)
    ]
    return jnp.concatenate(heads, axis=0)


def allowed_pairs(mark_ref, mark_all_ref, place_ref):
    rows, length = mark_ref.shape[1], mark_all_ref.shape[2]
    key_index = lax.broadcasted_iota(jnp.int32, (rows, length), 1)
    allowed = (key_index <= place_ref[...]) & (mark_all_ref[0] == mark_ref[0])
    bias = jnp.where(allowed, 0.0, 1.0)
    return jnp.concatenate([bias] * RATIO, axis=0) > 0.5


def probabilities(queries, keys, hidden_pairs):
    scores = against(queries, keys) * HEAD_DIM ** (-0.5)
    scores = jnp.where(hidden_pairs, MASKED, scores)
    weights = jnp.exp(scores - jnp.max(scores, axis=1, keepdims=True))
    return weights * (1.0 / jnp.sum(weights, axis=1, keepdims=True))


def attend_kernel(query_ref, pack_ref, mark_ref, mark_all_ref, place_ref, mixed_ref):
    rows = query_ref.shape[1]
    hidden_pairs = allowed_pairs(mark_ref, mark_all_ref, place_ref)
    for group in range(KV_HEADS):
        begin = group * HEAD_DIM
        keys = pack_ref[0, :, begin : begin + HEAD_DIM]
        values = pack_ref[0, :, KEY_WIDTH + begin : KEY_WIDTH + begin + HEAD_DIM]
        shares = probabilities(stacked_heads(query_ref, group), keys, hidden_pairs)
        mixed = jnp.dot(
            shares.astype(jnp.bfloat16), values, preferred_element_type=jnp.float32
        ).astype(jnp.bfloat16)
        for head in range(RATIO):
            place = (group * RATIO + head) * HEAD_DIM
            mixed_ref[0, :, place : place + HEAD_DIM] = mixed[head * rows : (head + 1) * rows]


def attend_back_kernel(
    query_ref, pack_ref, mark_ref, mark_all_ref, place_ref, back_ref, back_query_ref, back_pack_ref
):
    rows = query_ref.shape[1]
    scale = HEAD_DIM ** (-0.5)
    hidden_pairs = allowed_pairs(mark_ref, mark_all_ref, place_ref)
    for group in range(KV_HEADS):
        begin = group * HEAD_DIM
        keys = pack_ref[0, :, begin : begin + HEAD_DIM]
        values = pack_ref[0, :, KEY_WIDTH + begin : KEY_WIDTH + begin + HEAD_DIM]
        queries = stacked_heads(query_ref, group)
        back = stacked_heads(back_ref, group)
        shares = probabilities(queries, keys, hidden_pairs)
        back_shares = against(back, values)
        delta = jnp.sum(shares * back_shares, axis=1, keepdims=True)
        back_scores = (shares * (back_shares - delta)).astype(jnp.bfloat16)
        back_values = inner_rows(shares.astype(jnp.bfloat16), back)
        back_keys = inner_rows(back_scores, queries) * scale
        back_queries = jnp.dot(back_scores, keys, preferred_element_type=jnp.float32) * scale
        back_pack_ref[0, :, begin : begin + HEAD_DIM] = back_keys.astype(jnp.bfloat16)
        back_pack_ref[0, :, KEY_WIDTH + begin : KEY_WIDTH + begin + HEAD_DIM] = back_values.astype(
            jnp.bfloat16
        )
        for head in range(RATIO):
            place = (group * RATIO + head) * HEAD_DIM
            back_query_ref[0, :, place : place + HEAD_DIM] = back_queries[
                head * rows : (head + 1) * rows
            ]


def sequence_spec(shape):
    return pl.BlockSpec((1,) + tuple(shape[1:]), lambda index: (index, 0, 0))


def attention_call(kernel, queries, gathered, mark, mark_all, query_index, extra, outs, products):
    count, rows, width = queries.shape
    length = gathered.shape[1]
    operands = (
        queries,
        gathered,
        mark.astype(jnp.float32)[:, :, None],
        mark_all.astype(jnp.float32)[:, None, :],
        query_index[:, None],
    ) + extra
    in_specs = [sequence_spec(operand.shape) for operand in operands]
    in_specs[4] = pl.BlockSpec((rows, 1), lambda index: (0, 0))
    pairs = count * HEADS * rows * length
    return pl.pallas_call(
        kernel,
        grid=(count,),
        in_specs=in_specs,
        out_specs=[sequence_spec(out.shape) for out in outs],
        out_shape=outs,
        compiler_params=pltpu.CompilerParams(vmem_limit_bytes=48 * 1024 * 1024),
        cost_estimate=pl.CostEstimate(
            flops=2 * products * pairs * HEAD_DIM,
            bytes_accessed=4 * (gathered.size + queries.size),
            transcendentals=pairs,
        ),
    )(*operands)


def attend(queries, gathered, mark, mark_all, query_index):
    outs = [jax.ShapeDtypeStruct(queries.shape, jnp.bfloat16)]
    return attention_call(
        attend_kernel, queries, gathered, mark, mark_all, query_index, (), outs, 2
    )[0]


def attend_back(queries, gathered, mark, mark_all, query_index, back):
    outs = [
        jax.ShapeDtypeStruct(queries.shape, jnp.float32),
        jax.ShapeDtypeStruct(gathered.shape, jnp.bfloat16),
    ]
    return attention_call(
        attend_back_kernel, queries, gathered, mark, mark_all, query_index, (back,), outs, 5
    )


def times(left, halves):
    pieces = [
        jnp.dot(left, halves[part], preferred_element_type=jnp.float32)
        for part in range(halves.shape[0])
    ]
    return jnp.concatenate(pieces, axis=1)


def times_back(left, halves):
    lanes = halves.shape[2]
    total = against(left[:, :lanes], halves[0])
    for part in range(1, halves.shape[0]):
        total = total + against(left[:, part * lanes : (part + 1) * lanes], halves[part])
    return total


def swap_halves(values):
    half = HEAD_DIM // 2
    width = values.shape[-1]
    lane = lax.broadcasted_iota(jnp.int32, values.shape, 1) % HEAD_DIM
    ahead = jnp.concatenate([values[:, half:], values[:, :half]], axis=1)
    behind = jnp.concatenate([values[:, width - half :], values[:, : width - half]], axis=1)
    return jnp.where(lane < half, ahead, behind)


def turn(values, cosine, sine):
    copies = values.shape[-1] // HEAD_DIM
    return values * jnp.tile(cosine, (1, copies)) + swap_halves(values) * jnp.tile(
        sine, (1, copies)
    )


def layer_forward(hidden, full, segment_mark, segment_all, cosine, sine, query_index):
    qkv_weight, out_weight, gate_weight, up_weight, down_weight, gains = full
    count, local_length = segment_mark.shape
    rows = hidden.shape[0]
    key_width = KV_HEADS * HEAD_DIM
    query_width = HEADS * HEAD_DIM
    scale_front, normed = normalize(hidden, gains[0])
    qkv = times_back(normed, qkv_weight)
    turned = turn(qkv[:, : query_width + key_width], cosine, sine).astype(jnp.bfloat16)
    values = qkv[:, query_width + key_width :].astype(jnp.bfloat16)
    packed = jnp.concatenate([turned[:, query_width:], values], axis=-1)
    gathered = lax.all_gather(
        packed.reshape(count, local_length, 2 * key_width), "seq", axis=1, tiled=True
    )
    query_view = turned[:, :query_width].reshape(count, local_length, query_width)
    mixed_low = attend(query_view, gathered, segment_mark, segment_all, query_index)
    mixed_low = mixed_low.reshape(rows, query_width)
    middle = hidden + times(mixed_low, out_weight)
    scale_back, normed_back = normalize(middle, gains[1])
    gate = times_back(normed_back, gate_weight)
    upward = times_back(normed_back, up_weight)
    product = (gate * jax.nn.sigmoid(gate) * upward).astype(jnp.bfloat16)
    output = middle + times(product, down_weight)
    kept = (
        hidden,
        scale_front,
        normed,
        query_view,
        gathered,
        mixed_low,
        middle,
        scale_back,
        normed_back,
        gate,
        upward,
        product,
    )
    return (output, kept)


def layer_backward(incoming_low, full, kept, segment_mark, segment_all, cosine, sine, query_index):
    qkv_weight, out_weight, gate_weight, up_weight, down_weight, gains = full
    (
        hidden,
        scale_front,
        normed,
        query_view,
        gathered,
        mixed_low,
        middle,
        scale_back,
        normed_back,
        gate,
        upward,
        product,
    ) = kept
    rows = hidden.shape[0]
    key_width = KV_HEADS * HEAD_DIM
    query_width = HEADS * HEAD_DIM
    incoming = incoming_low.astype(jnp.float32)
    back_product = times_back(incoming_low, down_weight)
    sigma = jax.nn.sigmoid(gate)
    back_gate = (back_product * upward * sigma * (1.0 + gate * (1.0 - sigma))).astype(jnp.bfloat16)
    back_up = (back_product * gate * sigma).astype(jnp.bfloat16)
    back_normed = times(back_gate, gate_weight) + times(back_up, up_weight)
    inward, gain_back_grad = norm_back(back_normed, middle, scale_back, gains[1])
    back_middle = incoming + inward
    branch = back_middle.astype(jnp.bfloat16)
    back_mixed = times_back(branch, out_weight).astype(jnp.bfloat16)
    back_view = back_mixed.reshape(query_view.shape)
    back_query, buffer = attend_back(
        query_view, gathered, segment_mark, segment_all, query_index, back_view
    )
    summed = lax.psum_scatter(
        buffer, "seq", scatter_dimension=1, tiled=True
    ).reshape(rows, 2 * key_width)
    back_queries = turn(back_query.reshape(rows, query_width), cosine, -sine).astype(jnp.bfloat16)
    back_keys = turn(summed[:, :key_width].astype(jnp.float32), cosine, -sine).astype(jnp.bfloat16)
    back_qkv = jnp.concatenate([back_queries, back_keys, summed[:, key_width:]], axis=1)
    back_front = times(back_qkv, qkv_weight)
    inward_front, gain_front_grad = norm_back(back_front, hidden, scale_front, gains[0])
    back_hidden = back_middle + inward_front
    gains_grad = jnp.stack([gain_front_grad, gain_back_grad])
    terms = (
        normed,
        back_qkv,
        mixed_low,
        branch,
        normed_back,
        back_gate,
        back_up,
        product,
        incoming_low,
    )
    return (back_hidden, terms, gains_grad)


GAIN_ROWS = 16


def gather_weights(shards):
    query_part, key_part, value_part, out_part, gate_part, up_part, down_part, gain_part = shards
    seq = lax.axis_size("seq")
    dp = lax.axis_size("dp")
    lanes = query_part.shape[0]
    heights = (query_part.shape[1], key_part.shape[1], value_part.shape[1], out_part.shape[0])
    gain_block = jnp.pad(
        gain_part, ((0, GAIN_ROWS - gain_part.shape[0]), (0, lanes - gain_part.shape[1]))
    )
    front = jnp.concatenate(
        [
            jnp.concatenate([query_part, key_part, value_part], axis=1).T,
            out_part,
            gain_block,
        ],
        axis=0,
    )
    step = gate_part.shape[1]
    rear = jnp.concatenate([gate_part, up_part], axis=1).T.reshape(2, step, lanes)
    rear = jnp.concatenate([rear, down_part[None]], axis=0)
    front_all = lax.all_gather(front, ("seq", "dp"), axis=0, tiled=False)
    front_all = front_all.reshape(seq, dp, front.shape[0], lanes)
    rear_all = lax.all_gather(rear, ("dp", "seq"), axis=1, tiled=True)
    rear_all = rear_all.reshape(3, dp, seq * step, lanes)

    def whole(block, begin, size):
        piece = lax.slice_in_dim(block, begin, begin + size, axis=2)
        return piece.transpose(1, 0, 2, 3).reshape(dp, seq * size, lanes)

    places = [0]
    for height in heights:
        places.append(places[-1] + height)
    qkv = jnp.concatenate([whole(front_all, places[i], heights[i]) for i in range(3)], axis=1)
    out = whole(front_all, places[3], heights[3])
    gain_width = gain_part.shape[1]
    gains = lax.slice(
        front_all, (0, 0, places[4], 0), (seq, 1, places[4] + gain_part.shape[0], gain_width)
    )
    gains = gains[:, 0].transpose(1, 0, 2).reshape(gain_part.shape[0], seq * gain_width)
    return (qkv, out, rear_all[0], rear_all[1], rear_all[2], gains.astype(jnp.float32))


def outer(left, right, dp):
    lanes = right.shape[1] // dp
    return [
        inner_rows(left, right[:, part * lanes : (part + 1) * lanes]).astype(jnp.bfloat16)
        for part in range(dp)
    ]


def reduce_grads(terms, gains_grad):
    normed, back_qkv, mixed_low, branch, normed_back, back_gate, back_up, product, incoming = terms
    seq = lax.axis_size("seq")
    dp = lax.axis_size("dp")
    key_width = KV_HEADS * HEAD_DIM
    query_width = HEADS * HEAD_DIM
    pairs = ((back_gate, normed_back), (back_up, normed_back), (product, incoming))
    pieces = [piece for left, right in pairs for piece in outer(left, right, dp)]
    hidden_width, lanes = pieces[0].shape
    rear = jnp.concatenate(pieces, axis=0).reshape(len(pairs), dp * hidden_width, lanes)
    rear = lax.psum_scatter(rear, ("dp", "seq"), scatter_dimension=1, tiled=True)
    rear = rear.astype(jnp.float32)
    qkv = jnp.stack(outer(back_qkv, normed, dp))
    out = jnp.stack(outer(mixed_low, branch, dp))
    gain_kinds, gain_all = gains_grad.shape
    gain_width = gain_all // seq
    gain_block = gains_grad.astype(jnp.bfloat16).reshape(gain_kinds, seq, gain_width)
    gain_block = gain_block.transpose(1, 0, 2)
    gain_block = jnp.pad(
        gain_block, ((0, 0), (0, GAIN_ROWS - gain_kinds), (0, lanes - gain_width))
    )
    gain_block = jnp.broadcast_to(gain_block[None], (dp, seq, GAIN_ROWS, lanes))

    def split_rows(block):
        return block.reshape(dp, seq, block.shape[1] // seq, lanes)

    front = jnp.concatenate(
        [
            split_rows(qkv[:, :query_width]),
            split_rows(qkv[:, query_width : query_width + key_width]),
            split_rows(qkv[:, query_width + key_width :]),
            split_rows(out),
            gain_block,
        ],
        axis=2,
    )
    height = front.shape[2]
    front = lax.psum_scatter(
        front.reshape(dp * seq * height, lanes), ("dp", "seq"), scatter_dimension=0, tiled=True
    ).astype(jnp.float32)
    query_rows = query_width // seq
    key_rows = key_width // seq
    first = query_rows + key_rows
    second = first + key_rows
    third = second + query_rows
    return (
        front[:query_rows].T,
        front[query_rows:first].T,
        front[first:second].T,
        front[second:third],
        rear[0].T,
        rear[1].T,
        rear[2],
        front[third : third + gain_kinds, :gain_width],
    )


def pick_section(section, early, late):

    def select(early_part, late_part):
        return jnp.where(section == 0, early_part, late_part)

    return jax.tree.map(select, early, late)


def on_device(
    ends,
    segments,
    positions,
    query_weights,
    key_weights,
    value_weights,
    out_weights,
    gate_weights,
    up_weights,
    down_weights,
    norm_gains,
):
    section = lax.axis_index("section")
    sections = lax.axis_size("section")
    count = SEQ_MB
    micro = segments.shape[0] // count
    local_length = segments.shape[1]
    rows = count * local_length
    ticks = micro + sections - 1
    query_index = lax.axis_index("seq") * local_length + jnp.arange(local_length)
    shards = (
        query_weights[0],
        key_weights[0],
        value_weights[0],
        out_weights[0],
        gate_weights[0],
        up_weights[0],
        down_weights[0],
        norm_gains[0],
    )
    full = gather_weights(shards)
    outside = ends[0].reshape(micro, rows, D)
    blank = jnp.zeros((rows, D), jnp.bfloat16)

    marks = segments.astype(jnp.bfloat16)
    marks_all = lax.all_gather(marks, "seq", axis=1, tiled=True)
    cosines, sines = rope_tables(positions.reshape(micro * rows))
    cosines = jnp.concatenate([cosines, cosines], axis=1)
    sines = jnp.concatenate([-sines, sines], axis=1)

    def batch_inputs(index):
        mark = lax.dynamic_slice_in_dim(marks, index * count, count, 0)
        mark_all = lax.dynamic_slice_in_dim(marks_all, index * count, count, 0)
        cosine = lax.dynamic_slice_in_dim(cosines, index * rows, rows, 0)
        sine = lax.dynamic_slice_in_dim(sines, index * rows, rows, 0)
        return (mark, mark_all, cosine, sine)

    received = blank
    results = []
    stores = []
    for tick in range(ticks):
        own = outside[tick] if tick < micro else blank
        source = jnp.where(section == 0, own, received)
        index = jnp.clip(tick - section, 0, micro - 1)
        mark, mark_all, cosine, sine = batch_inputs(index)
        output, kept = layer_forward(
            source.astype(jnp.float32), full, mark, mark_all, cosine, sine, query_index
        )
        sent = output.astype(jnp.bfloat16)
        results.append(sent)
        stores.append(kept)
        if tick + 1 < ticks:
            received = shifted(sent, "section", 1)
    received = blank
    sent_back = []
    collected = []
    gains_grad = 0.0
    for tick in range(ticks):
        own = outside[tick] if tick < micro else blank
        incoming = jnp.where(section == sections - 1, own, received)
        index = jnp.clip(tick - 1 + section, 0, micro - 1)
        mark, mark_all, cosine, sine = batch_inputs(index)
        kept = pick_section(section, stores[max(tick - 1, 0)], stores[min(tick + 1, ticks - 1)])
        back_hidden, terms, gains_part = layer_backward(
            incoming, full, kept, mark, mark_all, cosine, sine, query_index
        )
        collected.append(terms)
        gains_grad = gains_grad + gains_part
        sent = back_hidden.astype(jnp.bfloat16)
        sent_back.append(sent)
        if tick + 1 < ticks:
            received = shifted(sent, "section", -1)
    terms = tuple(jnp.concatenate(parts, axis=0) for parts in zip(*collected))
    totals = reduce_grads(terms, gains_grad)
    outputs_list = []
    grads_list = []
    for batch in range(micro):
        outputs_list.append(
            jnp.where(section == 0, results[batch], results[batch + 1]).reshape(
                count, local_length, D
            )
        )
        grads_list.append(
            jnp.where(section == 0, sent_back[batch + 1], sent_back[batch]).reshape(
                count, local_length, D
            )
        )
    activations = jnp.concatenate(outputs_list, axis=0)[None]
    input_grads = jnp.concatenate(grads_list, axis=0)[None]
    return (
        activations,
        input_grads,
        totals[0][None],
        totals[1][None],
        totals[2][None],
        totals[3][None],
        totals[4][None],
        totals[5][None],
        totals[6][None],
        totals[7][None],
    )


def solution(mesh):
    return jax.shard_map(
        on_device,
        mesh=mesh,
        in_specs=(
            P("section", "dp", "seq", None),
            P("dp", "seq"),
            P("dp", "seq"),
            P("section", "dp", "seq"),
            P("section", "dp", "seq"),
            P("section", "dp", "seq"),
            P("section", "seq", "dp"),
            P("section", "dp", "seq"),
            P("section", "dp", "seq"),
            P("section", "seq", "dp"),
            P("section", None, "seq"),
        ),
        out_specs=(
            P("section", "dp", "seq", None),
            P("section", "dp", "seq", None),
            P("section", "dp", "seq"),
            P("section", "dp", "seq"),
            P("section", "dp", "seq"),
            P("section", "seq", "dp"),
            P("section", "dp", "seq"),
            P("section", "dp", "seq"),
            P("section", "seq", "dp"),
            P("section", None, "seq"),
        ),
        check_vma=False,
    )
```
